128 devices in a mesh: dp: 32 (over x, y, core), space: 4 (over z).
Axes of the slice: x: 4, y: 4, z: 4, core: 2. Of those that a mesh axis runs over, the one named last changes fastest.
Arguments:
- features: bfloat16 [32, 8, 128, 512], P('dp', 'space'), may hold values from -6 to 6
- latent_bank: float32 [1024, 512], replicated, may hold values from -6 to 6
- latent_ids: int32 [32], P('dp'), may hold values from 0 to 1023
- conv_kernel: bfloat16 [3, 3, 512, 512], P(None, None, 'dp'), may hold values from -0.09375 to 0.09375
- style_one: float32 [512, 512], replicated, may hold values from -0.25 to 0.25
- bias_one: float32 [512], replicated, may hold values from 0.1 to 1.9
- style_two: float32 [512, 512], replicated, may hold values from -0.25 to 0.25
- bias_two: float32 [512], replicated, may hold values from 0.1 to 1.9
- rgb_weight: float32 [512, 3], replicated, may hold values from -0.25 to 0.25
- conv_bias: float32 [512], replicated, may hold values from -3 to 3
- direction: float32 [32, 3, 8, 128], P('dp', None, 'space'), may hold values from -60 to 60
- length_target: float32 [1], replicated, may hold values from 0.5 to 3
Outputs:
- kernel_grad: float32 [3, 3, 512, 512], P(None, None, 'dp')
- path_lengths: float32 [32], P('dp')
- new_target: float32 [1], replicated
The draws below stay inside these ranges and needn't reach their ends.
All inputs are finite; a program needn't handle non-finite values.
Results may differ from the reference program's by a relative error of at most 0.025.
Values may be sent and summed in bfloat16 or wider, within the bound.
No kernel may reach another device: no remote copies, remote signals or barrier semaphores. Data moves between devices by JAX's collectives and lax.ppermute only.
A program may use at most 64 MiB of HBM per device.

```python
import math
import jax
import jax.numpy as jnp
from jax import lax

C = 512
L = 512
COLS = 128
POOL = 1024
BATCH = 32
H = 8


def draw_direction(key, part):
    position = jnp.arange(BATCH, dtype=jnp.float32) / max(BATCH - 1, 1)
    values = jnp.clip(jax.random.normal(key, (BATCH, 3, H, COLS), jnp.float32), -6.0, 6.0)
    rising = jnp.exp(position * jnp.log(10.0))
    return values * rising[:, None, None, None]


def with_ends(values, rng, low, high):
    dims = values.shape
    index_at = [jax.random.randint(jax.random.fold_in(rng, axis), (), 0, dims[axis]) for axis in range(len(dims))]
    values = values.at[tuple(index_at)].set(low)
    longest = dims.index(max(dims))
    index_at[longest] = (index_at[longest] + 1) % dims[longest]
    return values.at[tuple(index_at)].set(high)


def level_of(stream_key, dims, split, low, largest):
    def one(dim, parts):
        heights = jax.random.uniform(jax.random.fold_in(jax.random.fold_in(stream_key, 6), dim), (parts,), jnp.float32, low / len(split), largest / len(split))
        return jnp.repeat(jnp.exp(heights), dims[dim] // parts).reshape((-1,) + (1,) * (len(dims) - dim - 1))

    factor_of = one(*split[0])
    for cut in split[1:]:
        factor_of = factor_of * one(*cut)
    return factor_of


def scatter_about(rng, shape, deviation, most, pieces=(), kind=jnp.bfloat16):
    values = deviation * jax.random.normal(rng, shape, jnp.float32)
    if pieces:
        values = values * level_of(rng, shape, pieces, -0.22, 0.18)
    return jnp.clip(values, -most, most).astype(kind)


def setup_inputs(seed: int = 0) -> dict:
    arg_keys = jax.random.split(jax.random.key(seed), 13)
    return {
        "features": scatter_about(arg_keys[0], (BATCH, H, COLS, C), 1.0, 6.0, ((0, 32), (1, 4))),
        "latent_bank": scatter_about(arg_keys[1], (POOL, L), 1.0, 6.0, (), jnp.float32),
        "latent_ids": with_ends(jax.random.randint(arg_keys[2], (BATCH,), 0, POOL), jax.random.fold_in(arg_keys[2], 1), 0, POOL - 1).astype(jnp.int32),
        "conv_kernel": scatter_about(arg_keys[3], (3, 3, C, C), (9 * C) ** -0.5, 0.09375, ((2, 32),)),
        "style_one": scatter_about(arg_keys[4], (L, C), L ** -0.5, 0.25, (), jnp.float32),
        "bias_one": jnp.clip(1.0 + 0.18 * jax.random.normal(arg_keys[5], (C,), jnp.float32), 0.1, 1.9),
        "style_two": scatter_about(arg_keys[6], (L, C), L ** -0.5, 0.25, (), jnp.float32),
        "bias_two": jnp.clip(1.0 + 0.18 * jax.random.normal(arg_keys[7], (C,), jnp.float32), 0.1, 1.9),
        "rgb_weight": scatter_about(arg_keys[8], (C, 3), C ** -0.5, 0.25, (), jnp.float32),
        "conv_bias": scatter_about(arg_keys[9], (C,), 0.5, 3.0, (), jnp.float32),
        "direction": draw_direction(jax.random.fold_in(arg_keys[12], 71), 0),
        "length_target": jnp.clip(jax.random.uniform(arg_keys[11], (1,), jnp.float32, 0.5, 3.0), 0.5, 3.0),
    }


PL_WEIGHT = 8.0
PL_DECAY = 0.5
SQRT_TWO = math.sqrt(2.0)
HIGHEST = lax.Precision.HIGHEST

def synth(padded, latent, kernel_full, params, target_dir, scaling):
    style_one, bias_one, style_two, bias_two, rgb_weight, conv_bias = params
    tile_rows = padded.shape[0] - 2
    tile_cols = padded.shape[1] - 2
    channels = padded.shape[2]
    style_in = jnp.dot(latent, style_one, precision=HIGHEST) + bias_one
    energy = lax.optimization_barrier(jnp.sum(kernel_full * kernel_full, axis=(0, 1)))
    demodulation = lax.rsqrt(jnp.dot(style_in * style_in, energy, precision=HIGHEST) + 1e-08)
    modulated = (kernel_full * style_in[None, None, :, None] * demodulation[None, None, None, :]).astype(jnp.bfloat16)
    hidden = jnp.zeros((tile_rows * tile_cols, modulated.shape[3]), jnp.float32) + conv_bias
    for row_off in range(3):
        for col_off in range(3):
            window = padded[row_off:row_off + tile_rows, col_off:col_off + tile_cols].reshape(tile_rows * tile_cols, channels)
            hidden = hidden + jnp.dot(window, modulated[row_off, col_off], preferred_element_type=jnp.float32)
    activated = ((0.6 * hidden + 0.4 * jnp.sqrt(hidden * hidden + 0.25)) * SQRT_TWO).astype(jnp.bfloat16)
    colour = jnp.dot(latent, style_two, precision=HIGHEST) + bias_two
    rgb_mod = (rgb_weight * colour[:, None]).astype(jnp.bfloat16)
    picture = jnp.dot(activated, rgb_mod, preferred_element_type=jnp.float32)
    return jnp.sum(picture * target_dir.reshape(3, tile_rows * tile_cols).T) * scaling

def reference(features, latent_bank, latent_ids, conv_kernel, style_one, bias_one, style_two, bias_two, rgb_weight, conv_bias, direction, length_target):
    padded = jnp.pad(features, ((0, 0), (1, 1), (1, 1), (0, 0)))
    latents = jnp.take(latent_bank, latent_ids, axis=0)
    scaling = 1.0 / math.sqrt(features.shape[1] * features.shape[2])
    kernel_full = conv_kernel.astype(jnp.float32)
    params = (style_one, bias_one, style_two, bias_two, rgb_weight, conv_bias)

    def one_grad(item):
        pad_one, latent, dir_one = item
        return jax.grad(synth, argnums=1)(pad_one, latent, kernel_full, params, dir_one, scaling)
    style_grads = lax.map(one_grad, (padded, latents, direction))
    lengths = jnp.sqrt(lax.optimization_barrier(jnp.sum(style_grads * style_grads, axis=1)) + 1e-08)
    target = length_target + PL_DECAY * (jnp.mean(lengths) - length_target)
    factor = 2.0 * PL_WEIGHT * (lengths - target) / lengths
    tangents = factor[:, None] * style_grads

    def accumulate(total, item):
        pad_one, latent, tangent, dir_one = item

        def along(kernel_var):
            return jax.jvp(lambda point: synth(pad_one, point, kernel_var, params, dir_one, scaling), (latent,), (tangent,))[1]
        return (total + jax.grad(along)(kernel_full), None)
    kernel_grad = lax.scan(accumulate, jnp.zeros_like(kernel_full), (padded, latents, tangents, direction))[0]
    return (kernel_grad, lengths, target)
```

```python
import functools
import math

import jax
import jax.numpy as jnp
from jax import lax
from jax.experimental import pallas as pl
from jax.experimental.pallas import tpu as pltpu
from jax.sharding import PartitionSpec as P

PL_WEIGHT = 8.0
PL_DECAY = 0.5
SQRT_TWO = math.sqrt(2.0)
F32 = jnp.float32
BF16 = jnp.bfloat16

CH = 512
OC = 128
NPOS = 1024
COLS = 128
NDP = 32
VMEM = pltpu.VMEM
SMEM = pltpu.SMEM


def full(space=VMEM):
    return pl.BlockSpec(memory_space=space)


def params(mib):
    return pltpu.CompilerParams(vmem_limit_bytes=mib * 1024 * 1024)


def dot(a, b):
    return jnp.dot(a, b, preferred_element_type=F32)


def lanes_of(row):
    return jnp.transpose(jnp.broadcast_to(row, (OC, row.shape[1])))


def row_of(lanes):
    return jnp.sum(jnp.transpose(lanes), axis=0, keepdims=True)


def styles_kernel(z_ref, id_ref, bank_ref, w1_ref, b1_ref, w2_ref, b2_ref, s_ref, c_ref, w_buf, sem):
    copy = pltpu.make_async_copy(bank_ref.at[pl.ds(id_ref[0], 1)], w_buf, sem)
    copy.start()
    copy.wait()
    z = z_ref[0]
    lo = pl.multiple_of(z * OC, OC)
    w = lanes_of(w_buf[...])
    for j in range(4):
        block = pl.ds(j * OC, OC)
        s_ref[:, block] = jnp.sum(w * w1_ref[:, block], axis=0, keepdims=True) + b1_ref[:, block]
    mine = pl.ds(lo, OC)
    c_ref[...] = jnp.sum(w * w2_ref[:, mine], axis=0, keepdims=True) + b2_ref[:, mine]


def image_kernel(z_ref, m0, m1, m2, m3, f_ref, ft_ref, d_ref, dt_ref):
    z = z_ref[0]
    zero = jnp.zeros((COLS, CH), BF16)
    f_ref[0:COLS, :] = zero
    f_ref[NPOS + COLS :, :] = zero
    ft_ref[:, 0:COLS] = jnp.zeros((CH, COLS), BF16)
    ft_ref[:, NPOS + COLS :] = jnp.zeros((CH, COLS), BF16)
    for k, m in enumerate((m0, m1, m2, m3)):
        at = pl.multiple_of(lax.rem(z + 4 - k, 4) * 256, 256)
        feat = m[0:256, :]
        f_ref[pl.ds(at + COLS, 256), :] = feat
        ft_ref[:, pl.ds(at + COLS, 256)] = jnp.transpose(feat)
        part = m[256:272, 0:256]
        d_ref[:, pl.ds(at, 256)] = part
        wide = jnp.concatenate([part.astype(F32), jnp.zeros((112, 256), F32)], axis=0)
        dt_ref[pl.ds(at, 256), :] = jnp.transpose(wide).astype(BF16)


def column():
    return lax.rem(lax.broadcasted_iota(jnp.int32, (NPOS, OC), 0), COLS)


def from_left(x):
    return jnp.where(column() == 0, 0.0, pltpu.roll(x, 1, 0))


def from_right(x):
    return jnp.where(column() == COLS - 1, 0.0, pltpu.roll(x, NPOS - 1, 0))


def tap(k_ref, t):
    return k_ref[:, t].reshape(CH, OC).astype(F32)


def conv(f_ref, mod_of):
    total = None
    for dy in range(3):
        part = dot(f_ref[dy * COLS : dy * COLS + NPOS, :], mod_of(dy))
        total = part if total is None else total + part
    return from_left(total[:, 0:OC]) + total[:, OC : 2 * OC] + from_right(total[:, 2 * OC :])


def spread(h):
    return jnp.concatenate([from_right(h), h, from_left(h)], axis=1).astype(BF16)


def colours_of(rgb_ref, colour, z):
    lo = pl.multiple_of(z * OC, OC)
    rgb = rgb_ref[:, pl.ds(lo, OC)]
    mod = (rgb * colour).astype(BF16).astype(F32)[0:3]
    return rgb, jnp.concatenate([mod, mod, mod, jnp.zeros((119, OC), F32)], axis=0).astype(BF16)


def first_kernel(
    z_ref, f_ref, ft_ref, d_ref, dt_ref, k_ref, s_ref, c_ref, rgb_ref, bias_ref, w1_ref, w2_ref,
    u_ref, pre_ref, ga_ref, gm_ref, e_ref, rows_ref,
):
    z = z_ref[0]
    lo = pl.multiple_of(z * OC, OC)
    scaling = 1.0 / math.sqrt(NPOS)
    energy = None
    for t in range(9):
        k = tap(k_ref, t)
        energy = k * k if energy is None else energy + k * k
    e_ref[...] = energy
    s = lanes_of(s_ref[...])
    demod = lax.rsqrt(jnp.sum(s * s * energy, axis=0, keepdims=True) + 1e-08)
    sd = s * demod

    def mod_of(dy):
        return jnp.concatenate([(tap(k_ref, 3 * dy + dx) * sd).astype(BF16) for dx in range(3)], axis=1)

    bare = conv(f_ref, mod_of)
    pre = bare + bias_ref[:, pl.ds(lo, OC)]
    pre_ref[...] = pre
    square = pre * pre + 0.25
    root = lax.rsqrt(square)
    act = ((0.6 * pre + 0.4 * (square * root)) * SQRT_TWO).astype(BF16)
    rgb, mix = colours_of(rgb_ref, c_ref[...], z)
    ga = (dot(dt_ref[...], mix) * scaling).astype(BF16)
    ga_ref[...] = ga
    h = ga.astype(F32) * ((0.6 + 0.4 * (pre * root)) * SQRT_TWO)
    parts = dot(d_ref[...], act)
    grad_mix = ((parts[0:3] + parts[3:6] + parts[6:9]) * scaling).astype(BF16).astype(F32)
    grad_colour = jnp.sum(grad_mix * rgb[0:3], axis=0, keepdims=True)
    grad_demod = jnp.sum(h * bare, axis=0, keepdims=True) / demod
    grad_q = -0.5 * demod * demod * demod * grad_demod
    hs = spread(h)
    along = None
    for dy in range(3):
        gm = dot(ft_ref[:, dy * COLS : dy * COLS + NPOS], hs).astype(BF16)
        gm_ref[dy] = gm
        gm = gm.astype(F32)
        for dx in range(3):
            term = tap(k_ref, 3 * dy + dx) * gm[:, dx * OC : (dx + 1) * OC]
            along = term if along is None else along + term
    grad_s = row_of(along * demod + 2.0 * s * energy * grad_q)
    total = jnp.broadcast_to(grad_colour, (CH, OC)) * w2_ref[:, pl.ds(lo, OC)]
    for j in range(4):
        total = total + w1_ref[:, j * OC : (j + 1) * OC] * grad_s[:, j * OC : (j + 1) * OC]
    u_ref[...] = row_of(total)
    rows_ref[0:1, :] = demod
    rows_ref[1:2, :] = grad_demod


def second_kernel(
    z_ref, u0, u1, u2, u3, f_ref, ft_ref, dt_ref, k_ref, s_ref, rgb_ref, bias_ref, w1_ref, w2_ref,
    pre_ref, ga_ref, gm_ref, e_ref, rows_ref,
    out_ref, len_ref, u_buf,
):
    z = z_ref[0]
    lo = pl.multiple_of(z * OC, OC)
    scaling = 1.0 / math.sqrt(NPOS)
    for k, u in enumerate((u0, u1, u2, u3)):
        u_buf[pl.ds(lax.rem(z + 4 - k, 4), 1), :] = u[...]
    grad = (u_buf[0:1, :] + u_buf[1:2, :]) + (u_buf[2:3, :] + u_buf[3:4, :])
    length = jnp.sqrt(jnp.sum(grad * grad, axis=1, keepdims=True) + 1e-08)
    len_ref[...] = jnp.broadcast_to(length, (8, OC))
    point = lanes_of(grad)
    ds = lanes_of(
        jnp.concatenate(
            [jnp.sum(point * w1_ref[:, j * OC : (j + 1) * OC], axis=0, keepdims=True) for j in range(4)], axis=1
        )
    )
    dc = jnp.sum(point * w2_ref[:, pl.ds(lo, OC)], axis=0, keepdims=True)
    s = lanes_of(s_ref[...])
    energy = e_ref[...]
    demod = rows_ref[0:1, :]
    grad_demod = rows_ref[1:2, :]
    cube = demod * demod * demod
    dq = jnp.sum(2.0 * s * ds * energy, axis=0, keepdims=True)
    dd = -0.5 * cube * dq
    sd = s * demod
    dsd = ds * demod + s * dd

    def mod_of(dy):
        return jnp.concatenate([(tap(k_ref, 3 * dy + dx) * dsd).astype(BF16) for dx in range(3)], axis=1)

    dpre = conv(f_ref, mod_of)
    pre = pre_ref[...]
    root = lax.rsqrt(pre * pre + 0.25)
    slope = (0.6 + 0.4 * (pre * root)) * SQRT_TWO
    bend = (0.1 * SQRT_TWO) * (root * root * root)
    _, mix = colours_of(rgb_ref, dc, z)
    dga = (dot(dt_ref[...], mix) * scaling).astype(BF16).astype(F32)
    ga = ga_ref[...].astype(F32)
    h2 = ga * bend * dpre + dga * slope
    bare = pre - bias_ref[:, pl.ds(lo, OC)]
    cot_demod = (jnp.sum(h2 * bare + ga * slope * dpre, axis=0, keepdims=True) - dd * grad_demod) / demod
    cot_q = -0.5 * cube * cot_demod + 0.75 * cube * demod * demod * dq * grad_demod
    cot_dq = -0.5 * cube * grad_demod
    cot_e = 2.0 * s * (cot_q * s + 2.0 * cot_dq * ds)
    hs = spread(h2)
    for dy in range(3):
        gm2 = dot(ft_ref[:, dy * COLS : dy * COLS + NPOS], hs)
        for dx in range(3):
            t = 3 * dy + dx
            cut = slice(dx * OC, (dx + 1) * OC)
            value = gm2[:, cut] * sd + gm_ref[dy, :, cut].astype(F32) * dsd + tap(k_ref, t) * cot_e
            out_ref[:, t] = value.astype(BF16).reshape(NDP, 16, OC)
    high = length.astype(BF16)
    rest = length - high.astype(F32)
    middle = rest.astype(BF16)
    low = (rest - middle.astype(F32)).astype(BF16)
    row = lax.broadcasted_iota(jnp.int32, (16, OC), 0)
    pieces = jnp.where(row == 0, high.astype(F32), jnp.where(row == 1, middle.astype(F32), low.astype(F32)))
    out_ref[:, 9] = jnp.broadcast_to(pieces.astype(BF16)[None], (NDP, 16, OC))


def sum_kernel(part_ref, target_ref, out_ref, new_ref):
    lengths = []
    for b in range(NDP):
        tile = part_ref[b, 9].astype(F32)
        lengths.append(tile[0:1] + tile[1:2] + tile[2:3])
    total = lengths[0]
    for b in range(1, NDP):
        total = total + lengths[b]
    old = target_ref[0]
    target = old + PL_DECAY * (total / NDP - old)
    new_ref[...] = jnp.broadcast_to(target, (8, OC))
    value = None
    for b in range(NDP):
        factor = 2.0 * PL_WEIGHT * (lengths[b] - target) / lengths[b]
        term = part_ref[b, 0:9].astype(F32).reshape(144, OC) * factor
        value = term if value is None else value + term
    out_ref[...] = value.astype(BF16)


def last_kernel(z_ref, p0, p1, p2, p3, out_ref):
    z = z_ref[0]
    for k, p in enumerate((p0, p1, p2, p3)):
        at = pl.multiple_of(lax.rem(z + 4 - k, 4) * OC, OC)
        out_ref[:, pl.ds(at, OC)] = p[...].astype(F32)


def shape(dims, kind):
    return jax.ShapeDtypeStruct(dims, kind)


def call(kernel, outs, specs, mib, scratch=()):
    return pl.pallas_call(
        kernel,
        out_shape=outs,
        in_specs=specs,
        out_specs=jax.tree.map(lambda _: full(), outs),
        scratch_shapes=list(scratch),
        compiler_params=params(mib),
    )


def ring(x, axis, size):
    return [lax.ppermute(x, axis, [(i, (i + k) % size) for i in range(size)]) for k in range(1, size)]


def thirds(x):
    high = lax.reduce_precision(x, 8, 7)
    middle = lax.reduce_precision(x - high, 8, 7)
    return [high.astype(BF16), middle.astype(BF16), ((x - high) - middle).astype(BF16)]


def per_device(
    features, latent_bank, latent_ids, conv_kernel, style_one, bias_one, style_two, bias_two,
    rgb_weight, conv_bias, direction, length_target,
):
    zi = lax.axis_index("space")
    z = zi.reshape(1)
    mine = lax.dynamic_slice_in_dim(conv_kernel.reshape(9, 16, CH), zi * OC, OC, axis=2)
    kernel = lax.all_to_all(jnp.broadcast_to(mine[None], (NDP, 9, 16, OC)), "dp", 0, 0, tiled=True)
    marks = jnp.stack(thirds(direction.reshape(3, 256))).reshape(9, 256)
    message = jnp.concatenate([features.reshape(256, CH), jnp.pad(marks, ((0, 7), (0, 256)))], axis=0)
    others = ring(message, "space", 4)
    b1 = bias_one.reshape(1, CH)
    b2 = bias_two.reshape(1, CH)
    bias = conv_bias.reshape(1, CH)
    rgb = jnp.pad(rgb_weight.T, ((0, 5), (0, 0)))
    s, c = call(
        styles_kernel,
        (shape((1, CH), F32), shape((1, OC), F32)),
        [full(SMEM), full(SMEM), full(pl.ANY)] + [full()] * 4,
        16,
        [VMEM((1, CH), F32), pltpu.SemaphoreType.DMA],
    )(z, latent_ids, latent_bank, style_one, b1, style_two, b2)
    image, turned, marks_all, marks_turned = call(
        image_kernel,
        (shape((NPOS + 256, CH), BF16), shape((CH, NPOS + 256), BF16), shape((16, NPOS), BF16), shape((NPOS, OC), BF16)),
        [full(SMEM)] + [full()] * 4,
        24,
    )(z, message, *others)
    u, pre, ga, gm, energy, rows = call(
        first_kernel,
        (
            shape((1, CH), F32),
            shape((NPOS, OC), F32),
            shape((NPOS, OC), BF16),
            shape((3, CH, 3 * OC), BF16),
            shape((CH, OC), F32),
            shape((8, OC), F32),
        ),
        [full(SMEM)] + [full()] * 11,
        48,
    )(z, image, turned, marks_all, marks_turned, kernel, s, c, rgb, bias, style_one, style_two)
    parts, length = call(
        second_kernel,
        (shape((NDP, 10, 16, OC), BF16), shape((8, OC), F32)),
        [full(SMEM)] + [full()] * 18,
        48,
        [VMEM((8, CH), F32)],
    )(
        z, u, *ring(u, "space", 4), image, turned, marks_turned, kernel, s, rgb, bias, style_one, style_two,
        pre, ga, gm, energy, rows,
    )
    received = lax.all_to_all(parts, "dp", 0, 0, tiled=True)
    shard, target = call(
        sum_kernel,
        (shape((144, OC), BF16), shape((8, OC), F32)),
        [full(), full(SMEM)],
        16,
    )(received, length_target)
    kernel_grad = call(
        last_kernel,
        shape((144, CH), F32),
        [full(SMEM)] + [full()] * 4,
        16,
    )(z, shard, *ring(shard, "space", 4))
    return (kernel_grad.reshape(3, 3, 16, CH), length[0, 0:1], target[0, 0:1])


def solution(mesh):
    in_specs = (
        P("dp", "space", None, None),
        P(),
        P("dp"),
        P(None, None, "dp", None),
        P(),
        P(),
        P(),
        P(),
        P(),
        P(),
        P("dp", None, "space", None),
        P(),
    )
    out_specs = (P(None, None, "dp", None), P("dp"), P())
    return jax.shard_map(per_device, mesh=mesh, in_specs=in_specs, out_specs=out_specs, check_vma=False)
```

```python
import functools
import math

import jax
import jax.numpy as jnp
from jax import lax
from jax.experimental import pallas as pl
from jax.experimental.pallas import tpu as pltpu
from jax.sharding import PartitionSpec as P

PL_WEIGHT = 8.0
PL_DECAY = 0.5
SQRT_TWO = math.sqrt(2.0)
F32 = jnp.float32
BF16 = jnp.bfloat16

CH = 512
OC = 128
NPOS = 1024
COLS = 128
NDP = 32
VMEM = pltpu.VMEM
SMEM = pltpu.SMEM


def full(space=VMEM):
    return pl.BlockSpec(memory_space=space)


def params(mib):
    return pltpu.CompilerParams(vmem_limit_bytes=mib * 1024 * 1024)


def dot(a, b):
    return jnp.dot(a, b, preferred_element_type=F32)


def lanes_of(row):
    return jnp.transpose(jnp.broadcast_to(row, (OC, row.shape[1])))


def row_of(lanes):
    return jnp.sum(jnp.transpose(lanes), axis=0, keepdims=True)


def styles_kernel(z_ref, id_ref, bank_ref, w1_ref, b1_ref, w2_ref, b2_ref, s_ref, c_ref, w_buf, sem):
    copy = pltpu.make_async_copy(bank_ref.at[pl.ds(id_ref[0], 1)], w_buf, sem)
    copy.start()
    copy.wait()
    z = z_ref[0]
    lo = pl.multiple_of(z * OC, OC)
    w = lanes_of(w_buf[...])
    for j in range(4):
        block = pl.ds(j * OC, OC)
        s_ref[:, block] = jnp.sum(w * w1_ref[:, block], axis=0, keepdims=True) + b1_ref[:, block]
    mine = pl.ds(lo, OC)
    c_ref[...] = jnp.sum(w * w2_ref[:, mine], axis=0, keepdims=True) + b2_ref[:, mine]


def image_kernel(z_ref, m0, m1, m2, m3, arrived, f_ref, ft_ref, d_ref, dt_ref, held, sems):
    del arrived
    z = z_ref[0]
    copies = [pltpu.make_async_copy(m, held.at[k], sems.at[k]) for k, m in enumerate((m0, m1, m2, m3))]
    for copy in copies:
        copy.start()
    zero = jnp.zeros((COLS, CH), BF16)
    f_ref[0:COLS, :] = zero
    f_ref[NPOS + COLS :, :] = zero
    ft_ref[:, 0:COLS] = jnp.zeros((CH, COLS), BF16)
    ft_ref[:, NPOS + COLS :] = jnp.zeros((CH, COLS), BF16)
    for k, copy in enumerate(copies):
        copy.wait()
        m = held.at[k]
        at = pl.multiple_of(lax.rem(z + 4 - k, 4) * 256, 256)
        feat = m[0:256, :]
        f_ref[pl.ds(at + COLS, 256), :] = feat
        ft_ref[:, pl.ds(at + COLS, 256)] = jnp.transpose(feat)
        part = m[256:272, 0:256]
        d_ref[:, pl.ds(at, 256)] = part
        wide = jnp.concatenate([part.astype(F32), jnp.zeros((112, 256), F32)], axis=0)
        dt_ref[pl.ds(at, 256), :] = jnp.transpose(wide).astype(BF16)


def column():
    return lax.rem(lax.broadcasted_iota(jnp.int32, (NPOS, OC), 0), COLS)


def from_left(x):
    return jnp.where(column() == 0, 0.0, pltpu.roll(x, 1, 0))


def from_right(x):
    return jnp.where(column() == COLS - 1, 0.0, pltpu.roll(x, NPOS - 1, 0))


def tap(k_ref, t):
    return k_ref[:, t].reshape(CH, OC).astype(F32)


def conv(f_ref, mod_of):
    total = None
    for dy in range(3):
        part = dot(f_ref[dy * COLS : dy * COLS + NPOS, :], mod_of(dy))
        total = part if total is None else total + part
    return from_left(total[:, 0:OC]) + total[:, OC : 2 * OC] + from_right(total[:, 2 * OC :])


def spread(h):
    return jnp.concatenate([from_right(h), h, from_left(h)], axis=1).astype(BF16)


def colours_of(rgb_ref, colour, z):
    lo = pl.multiple_of(z * OC, OC)
    rgb = rgb_ref[:, pl.ds(lo, OC)]
    mod = (rgb * colour).astype(BF16).astype(F32)[0:3]
    return rgb, jnp.concatenate([mod, mod, mod, jnp.zeros((119, OC), F32)], axis=0).astype(BF16)


def first_kernel(
    z_ref, f_ref, ft_ref, d_ref, dt_ref, k_ref, s_ref, c_ref, rgb_ref, bias_ref, w1_ref, w2_ref,
    u_ref, pre_ref, ga_ref, gm_ref, e_ref, rows_ref,
):
    z = z_ref[0]
    lo = pl.multiple_of(z * OC, OC)
    scaling = 1.0 / math.sqrt(NPOS)
    energy = None
    for t in range(9):
        k = tap(k_ref, t)
        energy = k * k if energy is None else energy + k * k
    e_ref[...] = energy
    s = lanes_of(s_ref[...])
    demod = lax.rsqrt(jnp.sum(s * s * energy, axis=0, keepdims=True) + 1e-08)
    sd = s * demod

    def mod_of(dy):
        return jnp.concatenate([(tap(k_ref, 3 * dy + dx) * sd).astype(BF16) for dx in range(3)], axis=1)

    bare = conv(f_ref, mod_of)
    pre = bare + bias_ref[:, pl.ds(lo, OC)]
    pre_ref[...] = pre
    square = pre * pre + 0.25
    root = lax.rsqrt(square)
    act = ((0.6 * pre + 0.4 * (square * root)) * SQRT_TWO).astype(BF16)
    rgb, mix = colours_of(rgb_ref, c_ref[...], z)
    ga = (dot(dt_ref[...], mix) * scaling).astype(BF16)
    ga_ref[...] = ga
    h = ga.astype(F32) * ((0.6 + 0.4 * (pre * root)) * SQRT_TWO)
    parts = dot(d_ref[...], act)
    grad_mix = ((parts[0:3] + parts[3:6] + parts[6:9]) * scaling).astype(BF16).astype(F32)
    grad_colour = jnp.sum(grad_mix * rgb[0:3], axis=0, keepdims=True)
    grad_demod = jnp.sum(h * bare, axis=0, keepdims=True) / demod
    grad_q = -0.5 * demod * demod * demod * grad_demod
    hs = spread(h)
    along = None
    for dy in range(3):
        gm = dot(ft_ref[:, dy * COLS : dy * COLS + NPOS], hs).astype(BF16)
        gm_ref[dy] = gm
        gm = gm.astype(F32)
        for dx in range(3):
            term = tap(k_ref, 3 * dy + dx) * gm[:, dx * OC : (dx + 1) * OC]
            along = term if along is None else along + term
    grad_s = row_of(along * demod + 2.0 * s * energy * grad_q)
    total = jnp.broadcast_to(grad_colour, (CH, OC)) * w2_ref[:, pl.ds(lo, OC)]
    for j in range(4):
        total = total + w1_ref[:, j * OC : (j + 1) * OC] * grad_s[:, j * OC : (j + 1) * OC]
    u_ref[...] = row_of(total)
    rows_ref[0:1, :] = demod
    rows_ref[1:2, :] = grad_demod


def second_kernel(
    z_ref, u0, u1, u2, u3, f_ref, ft_ref, dt_ref, k_ref, s_ref, rgb_ref, bias_ref, w1_ref, w2_ref,
    pre_ref, ga_ref, gm_ref, e_ref, rows_ref,
    out_ref, len_ref, u_buf, parts, sems,
):
    z = z_ref[0]
    lo = pl.multiple_of(z * OC, OC)
    scaling = 1.0 / math.sqrt(NPOS)
    for k, u in enumerate((u0, u1, u2, u3)):
        u_buf[pl.ds(lax.rem(z + 4 - k, 4), 1), :] = u[...]
    grad = (u_buf[0:1, :] + u_buf[1:2, :]) + (u_buf[2:3, :] + u_buf[3:4, :])
    length = jnp.sqrt(jnp.sum(grad * grad, axis=1, keepdims=True) + 1e-08)
    len_ref[0] = length[0, 0]
    high = length.astype(BF16)
    rest = length - high.astype(F32)
    middle = rest.astype(BF16)
    low = (rest - middle.astype(F32)).astype(BF16)
    row = lax.broadcasted_iota(jnp.int32, (16, OC), 0)
    pieces = jnp.where(row == 0, high.astype(F32), jnp.where(row == 1, middle.astype(F32), low.astype(F32)))
    parts[:, 9] = jnp.broadcast_to(pieces.astype(BF16)[None], (NDP, 16, OC))
    copies = []
    for dy in range(3):
        some = pl.ds(3 * dy, 3)
        copies.append(pltpu.make_async_copy(parts.at[:, some], out_ref.at[:, some], sems.at[dy]))
    copies.append(pltpu.make_async_copy(parts.at[:, pl.ds(9, 1)], out_ref.at[:, pl.ds(9, 1)], sems.at[3]))
    copies[3].start()
    point = lanes_of(grad)
    ds = lanes_of(
        jnp.concatenate(
            [jnp.sum(point * w1_ref[:, j * OC : (j + 1) * OC], axis=0, keepdims=True) for j in range(4)], axis=1
        )
    )
    dc = jnp.sum(point * w2_ref[:, pl.ds(lo, OC)], axis=0, keepdims=True)
    s = lanes_of(s_ref[...])
    energy = e_ref[...]
    demod = rows_ref[0:1, :]
    grad_demod = rows_ref[1:2, :]
    cube = demod * demod * demod
    dq = jnp.sum(2.0 * s * ds * energy, axis=0, keepdims=True)
    dd = -0.5 * cube * dq
    sd = s * demod
    dsd = ds * demod + s * dd

    def mod_of(dy):
        return jnp.concatenate([(tap(k_ref, 3 * dy + dx) * dsd).astype(BF16) for dx in range(3)], axis=1)

    dpre = conv(f_ref, mod_of)
    pre = pre_ref[...]
    root = lax.rsqrt(pre * pre + 0.25)
    slope = (0.6 + 0.4 * (pre * root)) * SQRT_TWO
    bend = (0.1 * SQRT_TWO) * (root * root * root)
    _, mix = colours_of(rgb_ref, dc, z)
    dga = (dot(dt_ref[...], mix) * scaling).astype(BF16).astype(F32)
    ga = ga_ref[...].astype(F32)
    h2 = ga * bend * dpre + dga * slope
    bare = pre - bias_ref[:, pl.ds(lo, OC)]
    cot_demod = (jnp.sum(h2 * bare + ga * slope * dpre, axis=0, keepdims=True) - dd * grad_demod) / demod
    cot_q = -0.5 * cube * cot_demod + 0.75 * cube * demod * demod * dq * grad_demod
    cot_dq = -0.5 * cube * grad_demod
    cot_e = 2.0 * s * (cot_q * s + 2.0 * cot_dq * ds)
    hs = spread(h2)
    for dy in range(3):
        gm2 = dot(ft_ref[:, dy * COLS : dy * COLS + NPOS], hs)
        for dx in range(3):
            t = 3 * dy + dx
            cut = slice(dx * OC, (dx + 1) * OC)
            value = gm2[:, cut] * sd + gm_ref[dy, :, cut].astype(F32) * dsd + tap(k_ref, t) * cot_e
            parts[:, t] = value.astype(BF16).reshape(NDP, 16, OC)
        copies[dy].start()
    for copy in copies:
        copy.wait()


def sum_kernel(part_ref, target_ref, out_ref, new_ref):
    lengths = []
    for b in range(NDP):
        tile = part_ref[b, 9].astype(F32)
        lengths.append(tile[0:1] + tile[1:2] + tile[2:3])
    total = lengths[0]
    for b in range(1, NDP):
        total = total + lengths[b]
    old = target_ref[0]
    target = old + PL_DECAY * (total / NDP - old)
    new_ref[0] = target[0, 0]
    value = None
    for b in range(NDP):
        factor = 2.0 * PL_WEIGHT * (lengths[b] - target) / lengths[b]
        term = part_ref[b, 0:9].astype(F32).reshape(144, OC) * factor
        value = term if value is None else value + term
    out_ref[...] = value.astype(BF16)


def last_kernel(z_ref, p0, p1, p2, p3, out_ref):
    z = z_ref[0]
    for k, p in enumerate((p0, p1, p2, p3)):
        at = pl.multiple_of(lax.rem(z + 4 - k, 4) * OC, OC)
        out_ref[:, pl.ds(at, OC)] = p[...].astype(F32)


def shape(dims, kind):
    return jax.ShapeDtypeStruct(dims, kind)


def call(kernel, outs, specs, mib, scratch=(), out_specs=None):
    return pl.pallas_call(
        kernel,
        out_shape=outs,
        in_specs=specs,
        out_specs=out_specs or jax.tree.map(lambda _: full(), outs),
        scratch_shapes=list(scratch),
        compiler_params=params(mib),
    )


def ring(x, axis, size):
    return [lax.ppermute(x, axis, [(i, (i + k) % size) for i in range(size)]) for k in range(1, size)]


def thirds(x):
    high = lax.reduce_precision(x, 8, 7)
    middle = lax.reduce_precision(x - high, 8, 7)
    return [high.astype(BF16), middle.astype(BF16), ((x - high) - middle).astype(BF16)]


def per_device(
    features, latent_bank, latent_ids, conv_kernel, style_one, bias_one, style_two, bias_two,
    rgb_weight, conv_bias, direction, length_target,
):
    zi = lax.axis_index("space")
    z = zi.reshape(1)
    mine = lax.dynamic_slice_in_dim(conv_kernel.reshape(9, 16, CH), zi * OC, OC, axis=2)
    kernel = lax.all_to_all(jnp.broadcast_to(mine[None], (NDP, 9, 16, OC)), "dp", 0, 0, tiled=True)
    marks = jnp.stack(thirds(direction.reshape(3, 256))).reshape(9, 256)
    message = jnp.concatenate([features.reshape(256, CH), jnp.pad(marks, ((0, 7), (0, 256)))], axis=0)
    others = ring(message, "space", 4)
    b1 = bias_one.reshape(1, CH)
    b2 = bias_two.reshape(1, CH)
    bias = conv_bias.reshape(1, CH)
    rgb = jnp.pad(rgb_weight.T, ((0, 5), (0, 0)))
    s, c = call(
        styles_kernel,
        (shape((1, CH), F32), shape((1, OC), F32)),
        [full(SMEM), full(SMEM), full(pltpu.HBM)] + [full()] * 4,
        8,
        [VMEM((1, CH), F32), pltpu.SemaphoreType.DMA],
    )(z, latent_ids, pltpu.with_memory_space_constraint(latent_bank, pltpu.HBM), style_one, b1, style_two, b2)
    image, turned, marks_all, marks_turned = call(
        image_kernel,
        (shape((NPOS + 256, CH), BF16), shape((CH, NPOS + 256), BF16), shape((16, NPOS), BF16), shape((NPOS, OC), BF16)),
        [full(SMEM)] + [full(pltpu.HBM)] * 4 + [full(pl.ANY)],
        16,
        [VMEM((4, 272, CH), BF16), pltpu.SemaphoreType.DMA((4,))],
    )(z, *[pltpu.with_memory_space_constraint(x, pltpu.HBM) for x in (message, *others)], kernel)
    u, pre, ga, gm, energy, rows = call(
        first_kernel,
        (
            shape((1, CH), F32),
            shape((NPOS, OC), F32),
            shape((NPOS, OC), BF16),
            shape((3, CH, 3 * OC), BF16),
            shape((CH, OC), F32),
            shape((8, OC), F32),
        ),
        [full(SMEM)] + [full()] * 11,
        16,
    )(z, image, turned, marks_all, marks_turned, kernel, s, c, rgb, bias, style_one, style_two)
    parts, length = call(
        second_kernel,
        (pltpu.HBM((NDP, 10, 16, OC), BF16), shape((1,), F32)),
        [full(SMEM)] + [full()] * 18,
        16,
        [VMEM((8, CH), F32), VMEM((NDP, 10, 16, OC), BF16), pltpu.SemaphoreType.DMA((4,))],
        (full(pltpu.HBM), full(SMEM)),
    )(
        z, u, *ring(u, "space", 4), image, turned, marks_turned, kernel, s, rgb, bias, style_one, style_two,
        pre, ga, gm, energy, rows,
    )
    received = lax.all_to_all(parts, "dp", 0, 0, tiled=True)
    shard, target = call(
        sum_kernel,
        (shape((144, OC), BF16), shape((1,), F32)),
        [full(), full(SMEM)],
        8,
        out_specs=(full(), full(SMEM)),
    )(received, length_target)
    kernel_grad = call(
        last_kernel,
        shape((144, CH), F32),
        [full(SMEM)] + [full()] * 4,
        16,
    )(z, shard, *ring(shard, "space", 4))
    return (kernel_grad.reshape(3, 3, 16, CH), length, target)


def solution(mesh):
    in_specs = (
        P("dp", "space", None, None),
        P(),
        P("dp"),
        P(None, None, "dp", None),
        P(),
        P(),
        P(),
        P(),
        P(),
        P(),
        P("dp", None, "space", None),
        P(),
    )
    out_specs = (P(None, None, "dp", None), P("dp"), P())
    return jax.shard_map(per_device, mesh=mesh, in_specs=in_specs, out_specs=out_specs, check_vma=False)
```

```python
import functools
import math

import jax
import jax.numpy as jnp
from jax import lax
from jax.experimental import pallas as pl
from jax.experimental.pallas import tpu as pltpu
from jax.sharding import PartitionSpec as P

PL_WEIGHT = 8.0
PL_DECAY = 0.5
SQRT_TWO = math.sqrt(2.0)
F32 = jnp.float32
BF16 = jnp.bfloat16

CH = 512
OC = 128
NPOS = 1024
COLS = 128
NDP = 32
VMEM = pltpu.VMEM
SMEM = pltpu.SMEM


def full(space=VMEM):
    return pl.BlockSpec(memory_space=space)


def params(mib):
    return pltpu.CompilerParams(vmem_limit_bytes=mib * 1024 * 1024)


def dot(a, b):
    return jnp.dot(a, b, preferred_element_type=F32)


def lanes_of(row):
    return jnp.transpose(jnp.broadcast_to(row, (OC, row.shape[1])))


def row_of(lanes):
    return jnp.sum(jnp.transpose(lanes), axis=0, keepdims=True)


def styles_kernel(z_ref, id_ref, bank_ref, w1_ref, b1_ref, w2_ref, b2_ref, s_ref, c_ref, w_buf, sem):
    copy = pltpu.make_async_copy(bank_ref.at[pl.ds(id_ref[0], 1)], w_buf, sem)
    copy.start()
    copy.wait()
    z = z_ref[0]
    lo = pl.multiple_of(z * OC, OC)
    w = lanes_of(w_buf[...])
    for j in range(4):
        block = pl.ds(j * OC, OC)
        s_ref[:, block] = jnp.sum(w * w1_ref[:, block], axis=0, keepdims=True) + b1_ref[:, block]
    mine = pl.ds(lo, OC)
    c_ref[...] = jnp.sum(w * w2_ref[:, mine], axis=0, keepdims=True) + b2_ref[:, mine]


def image_kernel(z_ref, m0, m1, m2, m3, f_ref, ft_ref, d_ref, dt_ref):
    z = z_ref[0]
    for k, m in enumerate((m0, m1, m2, m3)):
        at = pl.multiple_of(lax.rem(z + 4 - k, 4) * 256, 256)
        feat = m[0:256, :]
        f_ref[pl.ds(at, 256), :] = feat
        ft_ref[:, pl.ds(at, 256)] = jnp.transpose(feat)
        part = m[256:272, 0:256]
        d_ref[:, pl.ds(at, 256)] = part
        wide = jnp.concatenate([part.astype(F32), jnp.zeros((112, 256), F32)], axis=0)
        dt_ref[pl.ds(at, 256), :] = jnp.transpose(wide).astype(BF16)


def column():
    return lax.rem(lax.broadcasted_iota(jnp.int32, (NPOS, OC), 0), COLS)


def from_left(x):
    return jnp.where(column() == 0, 0.0, pltpu.roll(x, 1, 0))


def from_right(x):
    return jnp.where(column() == COLS - 1, 0.0, pltpu.roll(x, NPOS - 1, 0))


def tap(k_ref, t):
    return k_ref[:, t].reshape(CH, OC).astype(F32)


def from_above(x):
    return jnp.concatenate([jnp.zeros((COLS, x.shape[1]), x.dtype), x[: NPOS - COLS]], axis=0)


def from_below(x):
    return jnp.concatenate([x[COLS:], jnp.zeros((COLS, x.shape[1]), x.dtype)], axis=0)


def conv(f_ref, mod):
    every = dot(f_ref[...], mod)
    wide = 3 * OC
    total = from_above(every[:, :wide]) + every[:, wide : 2 * wide] + from_below(every[:, 2 * wide :])
    return from_left(total[:, 0:OC]) + total[:, OC : 2 * OC] + from_right(total[:, 2 * OC :])


def spread(h):
    row = jnp.concatenate([from_right(h), h, from_left(h)], axis=1).astype(BF16)
    return jnp.concatenate([from_below(row), row, from_above(row)], axis=1)


def colours_of(rgb_ref, colour, z):
    lo = pl.multiple_of(z * OC, OC)
    rgb = rgb_ref[:, pl.ds(lo, OC)]
    mod = (rgb * colour).astype(BF16).astype(F32)[0:3]
    return rgb, jnp.concatenate([mod, mod, mod, jnp.zeros((119, OC), F32)], axis=0).astype(BF16)


def first_kernel(
    z_ref, p_ref, f_ref, ft_ref, d_ref, dt_ref, k0_ref, k1_ref, s_ref, c_ref, rgb_ref, bias_ref, w1_ref, w2_ref,
    k_ref, u_ref, pre_ref, ga_ref, gm_ref, e_ref, rows_ref,
):
    z = z_ref[0]
    lo = pl.multiple_of(z * OC, OC)
    scaling = 1.0 / math.sqrt(NPOS)
    core = lax.rem(p_ref[0], 2)
    for x in range(4):
        for y in range(4):
            chip = 8 * x + 2 * y
            k_ref[chip + core] = k0_ref[x, y]
            k_ref[chip + 1 - core] = k1_ref[x, y]
    energy = None
    for t in range(9):
        k = tap(k_ref, t)
        energy = k * k if energy is None else energy + k * k
    e_ref[...] = energy
    s = lanes_of(s_ref[...])
    demod = lax.rsqrt(jnp.sum(s * s * energy, axis=0, keepdims=True) + 1e-08)
    sd = s * demod

    mod = jnp.concatenate([(tap(k_ref, t) * sd).astype(BF16) for t in range(9)], axis=1)
    bare = conv(f_ref, mod)
    pre = bare + bias_ref[:, pl.ds(lo, OC)]
    pre_ref[...] = pre
    square = pre * pre + 0.25
    root = lax.rsqrt(square)
    act = ((0.6 * pre + 0.4 * (square * root)) * SQRT_TWO).astype(BF16)
    rgb, mix = colours_of(rgb_ref, c_ref[...], z)
    ga = (dot(dt_ref[...], mix) * scaling).astype(BF16)
    ga_ref[...] = ga
    h = ga.astype(F32) * ((0.6 + 0.4 * (pre * root)) * SQRT_TWO)
    parts = dot(d_ref[...], act)
    grad_mix = ((parts[0:3] + parts[3:6] + parts[6:9]) * scaling).astype(BF16).astype(F32)
    grad_colour = jnp.sum(grad_mix * rgb[0:3], axis=0, keepdims=True)
    grad_demod = jnp.sum(h * bare, axis=0, keepdims=True) / demod
    grad_q = -0.5 * demod * demod * demod * grad_demod
    hs = spread(h)
    along = None
    for dy in range(3):
        gm = dot(ft_ref[...], hs[:, 3 * OC * dy : 3 * OC * (dy + 1)]).astype(BF16)
        gm_ref[dy] = gm
        gm = gm.astype(F32)
        for dx in range(3):
            term = tap(k_ref, 3 * dy + dx) * gm[:, dx * OC : (dx + 1) * OC]
            along = term if along is None else along + term
    grad_s = row_of(along * demod + 2.0 * s * energy * grad_q)
    total = jnp.broadcast_to(grad_colour, (CH, OC)) * w2_ref[:, pl.ds(lo, OC)]
    for j in range(4):
        total = total + w1_ref[:, j * OC : (j + 1) * OC] * grad_s[:, j * OC : (j + 1) * OC]
    u_ref[...] = row_of(total)
    rows_ref[0:1, :] = demod
    rows_ref[1:2, :] = grad_demod


def second_kernel(
    z_ref, u0, u1, u2, u3, f_ref, ft_ref, dt_ref, k_ref, s_ref, rgb_ref, bias_ref, w1_ref, w2_ref,
    pre_ref, ga_ref, gm_ref, e_ref, rows_ref,
    out_ref, len_ref, u_buf, parts, sems,
):
    z = z_ref[0]
    lo = pl.multiple_of(z * OC, OC)
    scaling = 1.0 / math.sqrt(NPOS)
    for k, u in enumerate((u0, u1, u2, u3)):
        u_buf[pl.ds(lax.rem(z + 4 - k, 4), 1), :] = u[...]
    grad = (u_buf[0:1, :] + u_buf[1:2, :]) + (u_buf[2:3, :] + u_buf[3:4, :])
    length = jnp.sqrt(jnp.sum(grad * grad, axis=1, keepdims=True) + 1e-08)
    len_ref[...] = jnp.broadcast_to(length, (8, OC))
    high = length.astype(BF16)
    rest = length - high.astype(F32)
    middle = rest.astype(BF16)
    low = (rest - middle.astype(F32)).astype(BF16)
    row = lax.broadcasted_iota(jnp.int32, (16, OC), 0)
    pieces = jnp.where(row == 0, high.astype(F32), jnp.where(row == 1, middle.astype(F32), low.astype(F32)))
    parts[:, 9] = jnp.broadcast_to(pieces.astype(BF16)[None], (NDP, 16, OC))
    copies = []
    for dy in range(3):
        some = pl.ds(3 * dy, 3)
        copies.append(pltpu.make_async_copy(parts.at[:, some], out_ref.at[:, some], sems.at[dy]))
    copies.append(pltpu.make_async_copy(parts.at[:, pl.ds(9, 1)], out_ref.at[:, pl.ds(9, 1)], sems.at[3]))
    copies[3].start()
    point = lanes_of(grad)
    ds = lanes_of(
        jnp.concatenate(
            [jnp.sum(point * w1_ref[:, j * OC : (j + 1) * OC], axis=0, keepdims=True) for j in range(4)], axis=1
        )
    )
    dc = jnp.sum(point * w2_ref[:, pl.ds(lo, OC)], axis=0, keepdims=True)
    s = lanes_of(s_ref[...])
    energy = e_ref[...]
    demod = rows_ref[0:1, :]
    grad_demod = rows_ref[1:2, :]
    cube = demod * demod * demod
    dq = jnp.sum(2.0 * s * ds * energy, axis=0, keepdims=True)
    dd = -0.5 * cube * dq
    sd = s * demod
    dsd = ds * demod + s * dd

    mod = jnp.concatenate([(tap(k_ref, t) * dsd).astype(BF16) for t in range(9)], axis=1)
    dpre = conv(f_ref, mod)
    pre = pre_ref[...]
    root = lax.rsqrt(pre * pre + 0.25)
    slope = (0.6 + 0.4 * (pre * root)) * SQRT_TWO
    bend = (0.1 * SQRT_TWO) * (root * root * root)
    _, mix = colours_of(rgb_ref, dc, z)
    dga = (dot(dt_ref[...], mix) * scaling).astype(BF16).astype(F32)
    ga = ga_ref[...].astype(F32)
    h2 = ga * bend * dpre + dga * slope
    bare = pre - bias_ref[:, pl.ds(lo, OC)]
    cot_demod = (jnp.sum(h2 * bare + ga * slope * dpre, axis=0, keepdims=True) - dd * grad_demod) / demod
    cot_q = -0.5 * cube * cot_demod + 0.75 * cube * demod * demod * dq * grad_demod
    cot_dq = -0.5 * cube * grad_demod
    cot_e = 2.0 * s * (cot_q * s + 2.0 * cot_dq * ds)
    hs = spread(h2)
    for dy in range(3):
        gm2 = dot(ft_ref[...], hs[:, 3 * OC * dy : 3 * OC * (dy + 1)])
        for dx in range(3):
            t = 3 * dy + dx
            cut = slice(dx * OC, (dx + 1) * OC)
            value = gm2[:, cut] * sd + gm_ref[dy, :, cut].astype(F32) * dsd + tap(k_ref, t) * cot_e
            parts[:, t] = value.astype(BF16).reshape(NDP, 16, OC)
        copies[dy].start()
    for copy in copies:
        copy.wait()


def sum_kernel(part_ref, target_ref, out_ref, new_ref):
    lengths = []
    for b in range(NDP):
        tile = part_ref[b, 9].astype(F32)
        lengths.append(tile[0:1] + tile[1:2] + tile[2:3])
    total = lengths[0]
    for b in range(1, NDP):
        total = total + lengths[b]
    old = target_ref[0]
    target = old + PL_DECAY * (total / NDP - old)
    new_ref[...] = jnp.broadcast_to(target, (8, OC))
    value = None
    for b in range(NDP):
        factor = 2.0 * PL_WEIGHT * (lengths[b] - target) / lengths[b]
        term = part_ref[b, 0:9].astype(F32).reshape(144, OC) * factor
        value = term if value is None else value + term
    out_ref[...] = value.astype(BF16)


def last_kernel(z_ref, p0, p1, p2, p3, out_ref):
    z = z_ref[0]
    for k, p in enumerate((p0, p1, p2, p3)):
        at = pl.multiple_of(lax.rem(z + 4 - k, 4) * OC, OC)
        out_ref[:, pl.ds(at, OC)] = p[...].astype(F32)


def shape(dims, kind):
    return jax.ShapeDtypeStruct(dims, kind)


def call(kernel, outs, specs, mib, scratch=(), out_specs=None):
    return pl.pallas_call(
        kernel,
        out_shape=outs,
        in_specs=specs,
        out_specs=out_specs or jax.tree.map(lambda _: full(), outs),
        scratch_shapes=list(scratch),
        compiler_params=params(mib),
    )


def ring(x, axis, size):
    return [lax.ppermute(x, axis, [(i, (i + k) % size) for i in range(size)]) for k in range(1, size)]


def place(x, y, c):
    return ((x % 4) * 4 + y % 4) * 2 + c % 2


def permuted(value, to):
    return [
        lax.ppermute(
            value, "dp", [(place(x, y, c), place(*to(x, y, c, k))) for x in range(4) for y in range(4) for c in range(2)]
        )
        for k in range(1, 4)
    ]


def pack_kernel(z_ref, f_ref, d_hbm, k_ref, message_ref, mine_ref, d_ref, sems):
    lo = pl.multiple_of(z_ref[0] * OC, OC)
    copies = [
        pltpu.make_async_copy(f_ref, message_ref.at[pl.ds(0, 256)], sems.at[0]),
        pltpu.make_async_copy(k_ref.at[:, :, pl.ds(lo, OC)], mine_ref, sems.at[1]),
    ]
    marks = pltpu.make_async_copy(d_hbm, d_ref, sems.at[2])
    marks.start()
    for copy in copies:
        copy.start()
    marks.wait()
    rows = jnp.concatenate([d_ref[:, 0], d_ref[:, 1]], axis=1)
    high = rows.astype(BF16).astype(F32)
    middle = (rows - high).astype(BF16).astype(F32)
    low = (rows - high) - middle
    parts = jnp.concatenate([high, middle, low, jnp.zeros((7, 256), F32)], axis=0).astype(BF16)
    message_ref[256:272, :] = jnp.concatenate([parts, jnp.zeros((16, 256), BF16)], axis=1)
    for copy in copies:
        copy.wait()


def stack_kernel(step, p_ref, own, r1, r2, r3, *rest):
    out_ref = rest[-1]
    at = lax.rem(lax.div(p_ref[0], step), 4)
    for k, part in enumerate((own, r1, r2, r3)):
        out_ref[lax.rem(at + 4 - k, 4)] = part[...]


def stacked(place_of, step, own, parts, arrived):
    return call(
        functools.partial(stack_kernel, step),
        shape((4,) + own.shape, BF16),
        [full(SMEM)] + [full()] * 4 + [full(pl.ANY)] * len(arrived),
        8,
    )(place_of, own, *parts, *arrived)


def per_device(
    features, latent_bank, latent_ids, conv_kernel, style_one, bias_one, style_two, bias_two,
    rgb_weight, conv_bias, direction, length_target,
):
    zi = lax.axis_index("space")
    z = zi.reshape(1)
    di = lax.axis_index("dp").reshape(1)
    message, mine = call(
        pack_kernel,
        (shape((272, CH), BF16), shape((9, 16, OC), BF16)),
        [full(SMEM)] + [full(pltpu.HBM)] * 3,
        8,
        [VMEM((3, 2, COLS), F32), pltpu.SemaphoreType.DMA((3,))],
    )(
        z,
        pltpu.with_memory_space_constraint(features.reshape(256, CH), pltpu.HBM),
        pltpu.with_memory_space_constraint(direction.reshape(3, 2, COLS), pltpu.HBM),
        pltpu.with_memory_space_constraint(conv_kernel.reshape(9, 16, CH), pltpu.HBM),
    )
    others = ring(message, "space", 4)
    column = stacked(di, 2, mine, permuted(mine, lambda x, y, c, k: (x, y + k, c)), others[:1])
    plane = stacked(di, 8, column, permuted(column, lambda x, y, c, k: (x + k, y, c)), others[1:])
    sibling = lax.ppermute(plane, "dp", [(i, i ^ 1) for i in range(NDP)])
    b1 = bias_one.reshape(1, CH)
    b2 = bias_two.reshape(1, CH)
    bias = conv_bias.reshape(1, CH)
    rgb = jnp.pad(rgb_weight.T, ((0, 5), (0, 0)))
    s, c = call(
        styles_kernel,
        (shape((1, CH), F32), shape((1, OC), F32)),
        [full(SMEM), full(SMEM), full(pltpu.HBM)] + [full()] * 4,
        8,
        [VMEM((1, CH), F32), pltpu.SemaphoreType.DMA],
    )(z, latent_ids, pltpu.with_memory_space_constraint(latent_bank, pltpu.HBM), style_one, b1, style_two, b2)
    image, turned, marks_all, marks_turned = call(
        image_kernel,
        (shape((NPOS, CH), BF16), shape((CH, NPOS), BF16), shape((16, NPOS), BF16), shape((NPOS, OC), BF16)),
        [full(SMEM)] + [full()] * 4,
        16,
    )(z, message, *others)
    kernel, u, pre, ga, gm, energy, rows = call(
        first_kernel,
        (
            shape((NDP, 9, 16, OC), BF16),
            shape((1, CH), F32),
            shape((NPOS, OC), F32),
            shape((NPOS, OC), BF16),
            shape((3, CH, 3 * OC), BF16),
            shape((CH, OC), F32),
            shape((8, OC), F32),
        ),
        [full(SMEM)] * 2 + [full()] * 12,
        16,
    )(z, di, image, turned, marks_all, marks_turned, plane, sibling, s, c, rgb, bias, style_one, style_two)
    parts, length = call(
        second_kernel,
        (pltpu.HBM((NDP, 10, 16, OC), BF16), shape((8, OC), F32)),
        [full(SMEM)] + [full()] * 18,
        16,
        [VMEM((8, CH), F32), VMEM((NDP, 10, 16, OC), BF16), pltpu.SemaphoreType.DMA((4,))],
        (full(pltpu.HBM), full()),
    )(
        z, u, *ring(u, "space", 4), image, turned, marks_turned, kernel, s, rgb, bias, style_one, style_two,
        pre, ga, gm, energy, rows,
    )
    received = lax.all_to_all(parts, "dp", 0, 0, tiled=True)
    shard, target = call(
        sum_kernel,
        (shape((144, OC), BF16), shape((8, OC), F32)),
        [full(), full(SMEM)],
        8,
    )(received, length_target)
    kernel_grad = call(
        last_kernel,
        shape((144, CH), F32),
        [full(SMEM)] + [full()] * 4,
        16,
    )(z, shard, *ring(shard, "space", 4))
    return (kernel_grad.reshape(3, 3, 16, CH), length[0, 0:1], target[0, 0:1])


def solution(mesh):
    in_specs = (
        P("dp", "space", None, None),
        P(),
        P("dp"),
        P(None, None, "dp", None),
        P(),
        P(),
        P(),
        P(),
        P(),
        P(),
        P("dp", None, "space", None),
        P(),
    )
    out_specs = (P(None, None, "dp", None), P("dp"), P())
    return jax.shard_map(per_device, mesh=mesh, in_specs=in_specs, out_specs=out_specs, check_vma=False)
```

```python
import functools
import math

import jax
import jax.numpy as jnp
from jax import lax
from jax.experimental import pallas as pl
from jax.experimental.pallas import tpu as pltpu
from jax.sharding import PartitionSpec as P

PL_WEIGHT = 8.0
PL_DECAY = 0.5
SQRT_TWO = math.sqrt(2.0)
F32 = jnp.float32
BF16 = jnp.bfloat16

CH = 512
OC = 128
NPOS = 1024
COLS = 128
NDP = 32
VMEM = pltpu.VMEM
SMEM = pltpu.SMEM


def full(space=VMEM):
    return pl.BlockSpec(memory_space=space)


def params(mib):
    return pltpu.CompilerParams(vmem_limit_bytes=mib * 1024 * 1024)


def dot(a, b):
    return jnp.dot(a, b, preferred_element_type=F32)


def lanes_of(row):
    return jnp.transpose(jnp.broadcast_to(row, (OC, row.shape[1])))


def styles_kernel(
    z_ref, id_ref, bank_ref, w1_hbm, b1_ref, w2_hbm, b2_ref, s_ref, c_ref, w1t_ref, w2t_ref, w_buf, w1_ref, w2_ref, sems
):
    mine = pl.ds(pl.multiple_of(z_ref[0] * OC, OC), OC)
    copies = [
        pltpu.make_async_copy(bank_ref.at[pl.ds(id_ref[0], 1)], w_buf, sems.at[0]),
        pltpu.make_async_copy(w2_hbm.at[:, mine], w2_ref, sems.at[1]),
        pltpu.make_async_copy(w1_hbm, w1_ref, sems.at[2]),
    ]
    for copy in copies:
        copy.start()
    for copy in copies:
        copy.wait()
    w = lanes_of(w_buf[...])
    for j in range(4):
        block = pl.ds(j * OC, OC)
        s_ref[:, block] = jnp.sum(w * w1_ref[:, block], axis=0, keepdims=True) + b1_ref[:, block]
    c_ref[...] = jnp.sum(w * w2_ref[...], axis=0, keepdims=True) + b2_ref[:, mine]
    w1t_ref[...] = jnp.transpose(w1_ref[...])
    w2t_ref[...] = jnp.transpose(w2_ref[...])


def image_kernel(z_ref, m0, m1, m2, m3, f_ref, ft_ref, d_ref, dt_ref):
    z = z_ref[0]
    for k, m in enumerate((m0, m1, m2, m3)):
        at = pl.multiple_of(lax.rem(z + 4 - k, 4) * 256, 256)
        feat = m[0:256, :]
        f_ref[pl.ds(at, 256), :] = feat
        ft_ref[:, pl.ds(at, 256)] = jnp.transpose(feat)
        part = m[256:272, 0:256]
        d_ref[:, pl.ds(at, 256)] = part
        wide = jnp.concatenate([part.astype(F32), jnp.zeros((112, 256), F32)], axis=0)
        dt_ref[pl.ds(at, 256), :] = jnp.transpose(wide).astype(BF16)


def column():
    return lax.rem(lax.broadcasted_iota(jnp.int32, (NPOS, OC), 0), COLS)


def from_left(x):
    return jnp.where(column() == 0, 0.0, pltpu.roll(x, 1, 0))


def from_right(x):
    return jnp.where(column() == COLS - 1, 0.0, pltpu.roll(x, NPOS - 1, 0))


def tap(k_ref, t):
    return k_ref[:, t].reshape(CH, OC).astype(F32)


def from_above(x):
    return jnp.concatenate([jnp.zeros((COLS, x.shape[1]), x.dtype), x[: NPOS - COLS]], axis=0)


def from_below(x):
    return jnp.concatenate([x[COLS:], jnp.zeros((COLS, x.shape[1]), x.dtype)], axis=0)


def conv(f_ref, mod):
    every = dot(f_ref[...], mod)
    wide = 3 * OC
    total = from_above(every[:, :wide]) + every[:, wide : 2 * wide] + from_below(every[:, 2 * wide :])
    return from_left(total[:, 0:OC]) + total[:, OC : 2 * OC] + from_right(total[:, 2 * OC :])


def spread(h):
    row = jnp.concatenate([from_right(h), h, from_left(h)], axis=1).astype(BF16)
    return jnp.concatenate([from_below(row), row, from_above(row)], axis=1)


def colours_of(rgb_ref, colour, z):
    lo = pl.multiple_of(z * OC, OC)
    rgb = rgb_ref[:, pl.ds(lo, OC)]
    mod = (rgb * colour).astype(BF16).astype(F32)[0:3]
    return rgb, jnp.concatenate([mod, mod, mod, jnp.zeros((119, OC), F32)], axis=0).astype(BF16)


def first_kernel(
    z_ref, p_ref, f_ref, ft_ref, d_ref, dt_ref, k0_ref, k1_ref, s_ref, c_ref, rgb_ref, bias_ref, w1t_ref, w2t_ref,
    k_ref, u_ref, pre_ref, ga_ref, gm_ref, e_ref, rows_ref,
):
    z = z_ref[0]
    lo = pl.multiple_of(z * OC, OC)
    scaling = 1.0 / math.sqrt(NPOS)
    core = lax.rem(p_ref[0], 2)
    for x in range(4):
        for y in range(4):
            chip = 8 * x + 2 * y
            k_ref[chip + core] = k0_ref[x, y]
            k_ref[chip + 1 - core] = k1_ref[x, y]
    energy = None
    for t in range(9):
        k = tap(k_ref, t)
        energy = k * k if energy is None else energy + k * k
    e_ref[...] = energy
    s = lanes_of(s_ref[...])
    demod = lax.rsqrt(jnp.sum(s * s * energy, axis=0, keepdims=True) + 1e-08)
    sd = s * demod

    mod = jnp.concatenate([(tap(k_ref, t) * sd).astype(BF16) for t in range(9)], axis=1)
    bare = conv(f_ref, mod)
    pre = bare + bias_ref[:, pl.ds(lo, OC)]
    pre_ref[...] = pre
    square = pre * pre + 0.25
    root = lax.rsqrt(square)
    act = ((0.6 * pre + 0.4 * (square * root)) * SQRT_TWO).astype(BF16)
    rgb, mix = colours_of(rgb_ref, c_ref[...], z)
    ga = (dot(dt_ref[...], mix) * scaling).astype(BF16)
    ga_ref[...] = ga
    h = ga.astype(F32) * ((0.6 + 0.4 * (pre * root)) * SQRT_TWO)
    parts = dot(d_ref[...], act)
    grad_mix = ((parts[0:3] + parts[3:6] + parts[6:9]) * scaling).astype(BF16).astype(F32)
    grad_colour = jnp.sum(grad_mix * rgb[0:3], axis=0, keepdims=True)
    grad_demod = jnp.sum(h * bare, axis=0, keepdims=True) / demod
    grad_q = -0.5 * demod * demod * demod * grad_demod
    hs = spread(h)
    along = None
    for dy in range(3):
        gm = dot(ft_ref[...], hs[:, 3 * OC * dy : 3 * OC * (dy + 1)])
        gm_ref[dy] = gm.astype(BF16)
        for dx in range(3):
            term = tap(k_ref, 3 * dy + dx) * gm[:, dx * OC : (dx + 1) * OC]
            along = term if along is None else along + term
    grad_s = jnp.sum(along * demod + 2.0 * s * energy * grad_q, axis=1, keepdims=True)
    colour_lanes = lanes_of(grad_colour)[:, 0:1]
    u_ref[...] = jnp.sum(w1t_ref[...] * grad_s, axis=0, keepdims=True) + jnp.sum(
        w2t_ref[...] * colour_lanes, axis=0, keepdims=True
    )
    rows_ref[0:1, :] = demod
    rows_ref[1:2, :] = grad_demod


def second_kernel(
    z_ref, u0, u1, u2, u3, f_ref, ft_ref, dt_ref, k_ref, s_ref, rgb_ref, bias_ref, w1t_ref, w2t_ref,
    pre_ref, ga_ref, gm_ref, e_ref, rows_ref,
    out_ref, len_ref, u_buf,
):
    z = z_ref[0]
    lo = pl.multiple_of(z * OC, OC)
    scaling = 1.0 / math.sqrt(NPOS)
    for k, u in enumerate((u0, u1, u2, u3)):
        u_buf[pl.ds(lax.rem(z + 4 - k, 4), 1), :] = u[...]
    grad = (u_buf[0:1, :] + u_buf[1:2, :]) + (u_buf[2:3, :] + u_buf[3:4, :])
    length = jnp.sqrt(jnp.sum(grad * grad, axis=1, keepdims=True) + 1e-08)
    len_ref[...] = jnp.broadcast_to(length, (8, OC))
    high = length.astype(BF16)
    rest = length - high.astype(F32)
    middle = rest.astype(BF16)
    low = (rest - middle.astype(F32)).astype(BF16)
    row = lax.broadcasted_iota(jnp.int32, (8, OC), 0)
    pieces = jnp.where(row == 0, high.astype(F32), jnp.where(row == 1, middle.astype(F32), low.astype(F32)))
    out_ref[:, 144:152] = jnp.broadcast_to(pieces.astype(BF16)[None], (NDP, 8, OC))
    ds = jnp.broadcast_to(jnp.sum(w1t_ref[...] * grad, axis=1, keepdims=True), (CH, OC))
    dc_lanes = jnp.broadcast_to(jnp.sum(w2t_ref[...] * grad, axis=1, keepdims=True), (OC, OC))
    dc = jnp.transpose(dc_lanes)[0:1, :]
    s = lanes_of(s_ref[...])
    energy = e_ref[...]
    demod = rows_ref[0:1, :]
    grad_demod = rows_ref[1:2, :]
    cube = demod * demod * demod
    dq = jnp.sum(2.0 * s * ds * energy, axis=0, keepdims=True)
    dd = -0.5 * cube * dq
    sd = s * demod
    dsd = ds * demod + s * dd

    mod = jnp.concatenate([(tap(k_ref, t) * dsd).astype(BF16) for t in range(9)], axis=1)
    dpre = conv(f_ref, mod)
    pre = pre_ref[...]
    root = lax.rsqrt(pre * pre + 0.25)
    slope = (0.6 + 0.4 * (pre * root)) * SQRT_TWO
    bend = (0.1 * SQRT_TWO) * (root * root * root)
    _, mix = colours_of(rgb_ref, dc, z)
    dga = (dot(dt_ref[...], mix) * scaling).astype(BF16).astype(F32)
    ga = ga_ref[...].astype(F32)
    h2 = ga * bend * dpre + dga * slope
    bare = pre - bias_ref[:, pl.ds(lo, OC)]
    cot_demod = (jnp.sum(h2 * bare + ga * slope * dpre, axis=0, keepdims=True) - dd * grad_demod) / demod
    cot_q = -0.5 * cube * cot_demod + 0.75 * cube * demod * demod * dq * grad_demod
    cot_dq = -0.5 * cube * grad_demod
    cot_e = 2.0 * s * (cot_q * s + 2.0 * cot_dq * ds)
    hs = spread(h2)
    for dy in range(3):
        gm2 = dot(ft_ref[...], hs[:, 3 * OC * dy : 3 * OC * (dy + 1)])
        for dx in range(3):
            t = 3 * dy + dx
            cut = slice(dx * OC, (dx + 1) * OC)
            value = gm2[:, cut] * sd + gm_ref[dy, :, cut].astype(F32) * dsd + tap(k_ref, t) * cot_e
            out_ref[:, 16 * t : 16 * (t + 1)] = value.astype(BF16).reshape(NDP, 16, OC)


def sum_kernel(part_ref, target_ref, out_ref, new_ref):
    lengths = []
    for b in range(NDP):
        tile = part_ref[b, 144:152].astype(F32)
        lengths.append(tile[0:1] + tile[1:2] + tile[2:3])
    total = lengths[0]
    for b in range(1, NDP):
        total = total + lengths[b]
    old = target_ref[0]
    target = old + PL_DECAY * (total / NDP - old)
    new_ref[...] = jnp.broadcast_to(target, (8, OC))
    value = None
    for b in range(NDP):
        factor = 2.0 * PL_WEIGHT * (lengths[b] - target) / lengths[b]
        term = part_ref[b, 0:144].astype(F32) * factor
        value = term if value is None else value + term
    out_ref[...] = value.astype(BF16)


def last_kernel(z_ref, p0, p1, p2, p3, out_ref):
    z = z_ref[0]
    for k, p in enumerate((p0, p1, p2, p3)):
        at = pl.multiple_of(lax.rem(z + 4 - k, 4) * OC, OC)
        out_ref[:, pl.ds(at, OC)] = p[...].astype(F32)


def shape(dims, kind):
    return jax.ShapeDtypeStruct(dims, kind)


def call(kernel, outs, specs, mib, scratch=(), out_specs=None):
    return pl.pallas_call(
        kernel,
        out_shape=outs,
        in_specs=specs,
        out_specs=out_specs or jax.tree.map(lambda _: full(), outs),
        scratch_shapes=list(scratch),
        compiler_params=params(mib),
    )


def ring(x, axis, size):
    return [lax.ppermute(x, axis, [(i, (i + k) % size) for i in range(size)]) for k in range(1, size)]


def pinned(x):
    return pltpu.with_memory_space_constraint(x, pltpu.HBM)


def place(x, y, c):
    return ((x % 4) * 4 + y % 4) * 2 + c % 2


def permuted(value, to):
    return [
        lax.ppermute(
            value, "dp", [(place(x, y, c), place(*to(x, y, c, k))) for x in range(4) for y in range(4) for c in range(2)]
        )
        for k in range(1, 4)
    ]


def pack_kernel(z_ref, f_ref, d_hbm, k_ref, message_ref, mine_ref, d_ref, sems):
    lo = pl.multiple_of(z_ref[0] * OC, OC)
    copies = [
        pltpu.make_async_copy(f_ref, message_ref.at[pl.ds(0, 256)], sems.at[0]),
        pltpu.make_async_copy(k_ref.at[:, :, pl.ds(lo, OC)], mine_ref, sems.at[1]),
    ]
    marks = pltpu.make_async_copy(d_hbm, d_ref, sems.at[2])
    marks.start()
    for copy in copies:
        copy.start()
    marks.wait()
    rows = jnp.concatenate([d_ref[:, 0], d_ref[:, 1]], axis=1)
    high = rows.astype(BF16).astype(F32)
    middle = (rows - high).astype(BF16).astype(F32)
    low = (rows - high) - middle
    parts = jnp.concatenate([high, middle, low, jnp.zeros((7, 256), F32)], axis=0).astype(BF16)
    message_ref[256:272, :] = jnp.concatenate([parts, jnp.zeros((16, 256), BF16)], axis=1)
    for copy in copies:
        copy.wait()


def stack_kernel(step, p_ref, own, r1, r2, r3, *rest):
    out_ref = rest[-1]
    at = lax.rem(lax.div(p_ref[0], step), 4)
    for k, part in enumerate((own, r1, r2, r3)):
        out_ref[lax.rem(at + 4 - k, 4)] = part[...]


def stacked(place_of, step, own, parts, arrived):
    return call(
        functools.partial(stack_kernel, step),
        shape((4,) + own.shape, BF16),
        [full(SMEM)] + [full()] * 4 + [full(pl.ANY)] * len(arrived),
        8,
    )(place_of, own, *parts, *arrived)


def per_device(
    features, latent_bank, latent_ids, conv_kernel, style_one, bias_one, style_two, bias_two,
    rgb_weight, conv_bias, direction, length_target,
):
    zi = lax.axis_index("space")
    z = zi.reshape(1)
    di = lax.axis_index("dp").reshape(1)
    message, mine = call(
        pack_kernel,
        (shape((272, CH), BF16), shape((9, 16, OC), BF16)),
        [full(SMEM)] + [full(pltpu.HBM)] * 3,
        8,
        [VMEM((3, 2, COLS), F32), pltpu.SemaphoreType.DMA((3,))],
    )(
        z,
        pinned(features.reshape(256, CH)),
        pltpu.with_memory_space_constraint(direction.reshape(3, 2, COLS), pltpu.HBM),
        pltpu.with_memory_space_constraint(conv_kernel.reshape(9, 16, CH), pltpu.HBM),
    )
    others = ring(message, "space", 4)
    column = stacked(di, 2, mine, permuted(mine, lambda x, y, c, k: (x, y + k, c)), [])
    b1 = bias_one.reshape(1, CH)
    b2 = bias_two.reshape(1, CH)
    bias = conv_bias.reshape(1, CH)
    rgb = jnp.pad(rgb_weight.T, ((0, 5), (0, 0)))
    s, c, w1t, w2t = call(
        styles_kernel,
        (shape((1, CH), F32), shape((1, OC), F32), shape((CH, CH), F32), shape((OC, CH), F32)),
        [full(SMEM), full(SMEM), full(pltpu.HBM), full(pltpu.HBM), full(), full(pltpu.HBM), full()],
        8,
        [VMEM((1, CH), F32), VMEM((CH, CH), F32), VMEM((CH, OC), F32), pltpu.SemaphoreType.DMA((3,))],
    )(z, latent_ids, pinned(latent_bank), pinned(style_one), b1, pinned(style_two), b2)
    image, turned, marks_all, marks_turned = call(
        image_kernel,
        (shape((NPOS, CH), BF16), shape((CH, NPOS), BF16), shape((16, NPOS), BF16), shape((NPOS, OC), BF16)),
        [full(SMEM)] + [full()] * 4,
        16,
    )(z, message, *others)
    plane = stacked(di, 8, column, permuted(column, lambda x, y, c, k: (x + k, y, c)), [s, marks_all])
    sibling = lax.ppermute(plane, "dp", [(i, i ^ 1) for i in range(NDP)])
    kernel, u, pre, ga, gm, energy, rows = call(
        first_kernel,
        (
            shape((NDP, 9, 16, OC), BF16),
            shape((1, CH), F32),
            shape((NPOS, OC), F32),
            shape((NPOS, OC), BF16),
            shape((3, CH, 3 * OC), BF16),
            shape((CH, OC), F32),
            shape((8, OC), F32),
        ),
        [full(SMEM)] * 2 + [full()] * 12,
        16,
    )(z, di, image, turned, marks_all, marks_turned, plane, sibling, s, c, rgb, bias, w1t, w2t)
    parts, length = call(
        second_kernel,
        (pltpu.HBM((NDP, 152, OC), BF16), shape((8, OC), F32)),
        [full(SMEM)] + [full()] * 18,
        16,
        [VMEM((8, CH), F32)],
    )(
        z, u, *ring(u, "space", 4), image, turned, marks_turned, kernel, s, rgb, bias, w1t, w2t,
        pre, ga, gm, energy, rows,
    )
    received = lax.all_to_all(parts, "dp", 0, 0, tiled=True)
    shard, target = call(
        sum_kernel,
        (shape((144, OC), BF16), shape((8, OC), F32)),
        [full(), full(SMEM)],
        8,
    )(received, length_target)
    kernel_grad = call(
        last_kernel,
        shape((144, CH), F32),
        [full(SMEM)] + [full()] * 4,
        16,
    )(z, shard, *ring(shard, "space", 4))
    return (kernel_grad.reshape(3, 3, 16, CH), length[0, 0:1], target[0, 0:1])


def solution(mesh):
    in_specs = (
        P("dp", "space", None, None),
        P(),
        P("dp"),
        P(None, None, "dp", None),
        P(),
        P(),
        P(),
        P(),
        P(),
        P(),
        P("dp", None, "space", None),
        P(),
    )
    out_specs = (P(None, None, "dp", None), P("dp"), P())
    return jax.shard_map(per_device, mesh=mesh, in_specs=in_specs, out_specs=out_specs, check_vma=False)
```

```python
import functools
import math

import jax
import jax.numpy as jnp
from jax import lax
from jax.experimental import pallas as pl
from jax.experimental.pallas import tpu as pltpu
from jax.sharding import PartitionSpec as P

PL_WEIGHT = 8.0
PL_DECAY = 0.5
SQRT_TWO = math.sqrt(2.0)
F32 = jnp.float32
BF16 = jnp.bfloat16

CH = 512
OC = 128
NPOS = 1024
COLS = 128
NDP = 32
VMEM = pltpu.VMEM
SMEM = pltpu.SMEM


def full(space=VMEM):
    return pl.BlockSpec(memory_space=space)


def params(mib):
    return pltpu.CompilerParams(vmem_limit_bytes=mib * 1024 * 1024)


def dot(a, b):
    return jnp.dot(a, b, preferred_element_type=F32)


def lanes_of(row):
    return jnp.transpose(jnp.broadcast_to(row, (OC, row.shape[1])))


def styles_kernel(
    z_ref, id_ref, bank_ref, w1_hbm, b1_hbm, w2_hbm, b2_hbm, s_ref, c_ref, w1t_ref, w2t_ref,
    w_buf, w1_ref, w2_ref, b1_ref, b2_ref, sems,
):
    mine = pl.ds(pl.multiple_of(z_ref[0] * OC, OC), OC)
    copies = [
        pltpu.make_async_copy(bank_ref.at[pl.ds(id_ref[0], 1)], w_buf, sems.at[0]),
        pltpu.make_async_copy(w2_hbm.at[:, mine], w2_ref, sems.at[1]),
        pltpu.make_async_copy(w1_hbm, w1_ref, sems.at[2]),
        pltpu.make_async_copy(b1_hbm, b1_ref, sems.at[3]),
        pltpu.make_async_copy(b2_hbm, b2_ref, sems.at[4]),
    ]
    for copy in copies:
        copy.start()
    for copy in copies:
        copy.wait()
    w = lanes_of(w_buf[...])
    for j in range(4):
        block = pl.ds(j * OC, OC)
        s_ref[:, block] = jnp.sum(w * w1_ref[:, block], axis=0, keepdims=True) + b1_ref[:, block]
    c_ref[...] = jnp.sum(w * w2_ref[...], axis=0, keepdims=True) + b2_ref[:, mine]
    w1t_ref[...] = jnp.transpose(w1_ref[...])
    w2t_ref[...] = jnp.transpose(w2_ref[...])


def image_kernel(z_ref, m0, m1, m2, m3, f_ref, ft_ref, d_ref, dt_ref):
    z = z_ref[0]
    for k, m in enumerate((m0, m1, m2, m3)):
        at = pl.multiple_of(lax.rem(z + 4 - k, 4) * 256, 256)
        feat = m[0:256, :]
        f_ref[pl.ds(at, 256), :] = feat
        ft_ref[:, pl.ds(at, 256)] = jnp.transpose(feat)
        part = m[256:272, 0:256]
        d_ref[:, pl.ds(at, 256)] = part
        wide = jnp.concatenate([part.astype(F32), jnp.zeros((112, 256), F32)], axis=0)
        dt_ref[pl.ds(at, 256), :] = jnp.transpose(wide).astype(BF16)


def column():
    return lax.rem(lax.broadcasted_iota(jnp.int32, (NPOS, OC), 0), COLS)


def from_left(x):
    return jnp.where(column() == 0, 0.0, pltpu.roll(x, 1, 0))


def from_right(x):
    return jnp.where(column() == COLS - 1, 0.0, pltpu.roll(x, NPOS - 1, 0))


def tap(k_ref, t):
    return k_ref[:, t].reshape(CH, OC).astype(F32)


def from_above(x):
    return jnp.concatenate([jnp.zeros((COLS, x.shape[1]), x.dtype), x[: NPOS - COLS]], axis=0)


def from_below(x):
    return jnp.concatenate([x[COLS:], jnp.zeros((COLS, x.shape[1]), x.dtype)], axis=0)


def conv(f_ref, mod):
    every = dot(f_ref[...], mod)
    wide = 3 * OC
    total = from_above(every[:, :wide]) + every[:, wide : 2 * wide] + from_below(every[:, 2 * wide :])
    return from_left(total[:, 0:OC]) + total[:, OC : 2 * OC] + from_right(total[:, 2 * OC :])


def spread(h):
    row = jnp.concatenate([from_right(h), h, from_left(h)], axis=1).astype(BF16)
    return jnp.concatenate([from_below(row), row, from_above(row)], axis=1)


def colours_of(rgb_ref, colour, z):
    lo = pl.multiple_of(z * OC, OC)
    rgb = rgb_ref[:, pl.ds(lo, OC)]
    mod = (rgb * colour).astype(BF16).astype(F32)[0:3]
    return rgb, jnp.concatenate([mod, mod, mod, jnp.zeros((119, OC), F32)], axis=0).astype(BF16)


def ahead_kernel(z_ref, dt_ref, c_ref, rgb_ref, k0_ref, ga_ref, half_ref):
    _, mix = colours_of(rgb_ref, c_ref[...], z_ref[0])
    ga_ref[...] = (dot(dt_ref[...], mix) * (1.0 / math.sqrt(NPOS))).astype(BF16)
    for x in range(4):
        for y in range(4):
            k = k0_ref[x, y].astype(F32)
            half_ref[4 * x + y] = jnp.sum(k * k, axis=0)


def first_kernel(
    z_ref, p_ref, f_ref, ft_ref, d_ref, ga_ref, half_ref, k0_ref, k1_ref, s_ref, rgb_ref, bias_ref, w1t_ref, w2t_ref,
    k_ref, u_ref, pre_ref, gm_ref, e_ref, rows_ref,
):
    z = z_ref[0]
    lo = pl.multiple_of(z * OC, OC)
    scaling = 1.0 / math.sqrt(NPOS)
    core = lax.rem(p_ref[0], 2)
    for x in range(4):
        for y in range(4):
            chip = 8 * x + 2 * y
            k_ref[chip + core] = k0_ref[x, y]
            k_ref[chip + 1 - core] = k1_ref[x, y]
            other = k1_ref[x, y].astype(F32)
            e_ref[chip + core] = half_ref[4 * x + y]
            e_ref[chip + 1 - core] = jnp.sum(other * other, axis=0)
    energy = e_ref[...].reshape(CH, OC)
    s = lanes_of(s_ref[...])
    demod = lax.rsqrt(jnp.sum(s * s * energy, axis=0, keepdims=True) + 1e-08)
    sd = s * demod

    mod = jnp.concatenate([(tap(k_ref, t) * sd).astype(BF16) for t in range(9)], axis=1)
    bare = conv(f_ref, mod)
    pre = bare + bias_ref[:, pl.ds(lo, OC)]
    pre_ref[...] = pre
    square = pre * pre + 0.25
    root = lax.rsqrt(square)
    act = ((0.6 * pre + 0.4 * (square * root)) * SQRT_TWO).astype(BF16)
    rgb = rgb_ref[:, pl.ds(lo, OC)]
    h = ga_ref[...].astype(F32) * ((0.6 + 0.4 * (pre * root)) * SQRT_TWO)
    parts = dot(d_ref[...], act)
    grad_mix = ((parts[0:3] + parts[3:6] + parts[6:9]) * scaling).astype(BF16).astype(F32)
    grad_colour = jnp.sum(grad_mix * rgb[0:3], axis=0, keepdims=True)
    grad_demod = jnp.sum(h * bare, axis=0, keepdims=True) / demod
    grad_q = -0.5 * demod * demod * demod * grad_demod
    hs = spread(h)
    along = None
    for dy in range(3):
        gm = dot(ft_ref[...], hs[:, 3 * OC * dy : 3 * OC * (dy + 1)])
        gm_ref[dy] = gm.astype(BF16)
        for dx in range(3):
            term = tap(k_ref, 3 * dy + dx) * gm[:, dx * OC : (dx + 1) * OC]
            along = term if along is None else along + term
    grad_s = jnp.sum(along * demod + 2.0 * s * energy * grad_q, axis=1, keepdims=True)
    colour_lanes = lanes_of(grad_colour)[:, 0:1]
    u_ref[...] = jnp.sum(w1t_ref[...] * grad_s, axis=0, keepdims=True) + jnp.sum(
        w2t_ref[...] * colour_lanes, axis=0, keepdims=True
    )
    rows_ref[0:1, :] = demod
    rows_ref[1:2, :] = grad_demod


def second_kernel(
    z_ref, u0, u1, u2, u3, f_ref, ft_ref, dt_ref, k_ref, s_ref, rgb_ref, bias_ref, w1t_ref, w2t_ref,
    pre_ref, ga_ref, gm_ref, e_ref, rows_ref,
    out_ref, len_ref, u_buf,
):
    z = z_ref[0]
    lo = pl.multiple_of(z * OC, OC)
    scaling = 1.0 / math.sqrt(NPOS)
    for k, u in enumerate((u0, u1, u2, u3)):
        u_buf[pl.ds(lax.rem(z + 4 - k, 4), 1), :] = u[...]
    grad = (u_buf[0:1, :] + u_buf[1:2, :]) + (u_buf[2:3, :] + u_buf[3:4, :])
    length = jnp.sqrt(jnp.sum(grad * grad, axis=1, keepdims=True) + 1e-08)
    len_ref[...] = jnp.broadcast_to(length, (8, OC))
    high = length.astype(BF16)
    rest = length - high.astype(F32)
    middle = rest.astype(BF16)
    low = (rest - middle.astype(F32)).astype(BF16)
    row = lax.broadcasted_iota(jnp.int32, (8, OC), 0)
    pieces = jnp.where(row == 0, high.astype(F32), jnp.where(row == 1, middle.astype(F32), low.astype(F32)))
    out_ref[:, 144:152] = jnp.broadcast_to(pieces.astype(BF16)[None], (NDP, 8, OC))
    ds = jnp.broadcast_to(jnp.sum(w1t_ref[...] * grad, axis=1, keepdims=True), (CH, OC))
    dc_lanes = jnp.broadcast_to(jnp.sum(w2t_ref[...] * grad, axis=1, keepdims=True), (OC, OC))
    dc = jnp.transpose(dc_lanes)[0:1, :]
    s = lanes_of(s_ref[...])
    energy = e_ref[...].reshape(CH, OC)
    demod = rows_ref[0:1, :]
    grad_demod = rows_ref[1:2, :]
    cube = demod * demod * demod
    dq = jnp.sum(2.0 * s * ds * energy, axis=0, keepdims=True)
    dd = -0.5 * cube * dq
    sd = s * demod
    dsd = ds * demod + s * dd

    mod = jnp.concatenate([(tap(k_ref, t) * dsd).astype(BF16) for t in range(9)], axis=1)
    dpre = conv(f_ref, mod)
    pre = pre_ref[...]
    root = lax.rsqrt(pre * pre + 0.25)
    slope = (0.6 + 0.4 * (pre * root)) * SQRT_TWO
    bend = (0.1 * SQRT_TWO) * (root * root * root)
    _, mix = colours_of(rgb_ref, dc, z)
    dga = (dot(dt_ref[...], mix) * scaling).astype(BF16).astype(F32)
    ga = ga_ref[...].astype(F32)
    h2 = ga * bend * dpre + dga * slope
    bare = pre - bias_ref[:, pl.ds(lo, OC)]
    cot_demod = (jnp.sum(h2 * bare + ga * slope * dpre, axis=0, keepdims=True) - dd * grad_demod) / demod
    cot_q = -0.5 * cube * cot_demod + 0.75 * cube * demod * demod * dq * grad_demod
    cot_dq = -0.5 * cube * grad_demod
    cot_e = 2.0 * s * (cot_q * s + 2.0 * cot_dq * ds)
    hs = spread(h2)
    for dy in range(3):
        gm2 = dot(ft_ref[...], hs[:, 3 * OC * dy : 3 * OC * (dy + 1)])
        for dx in range(3):
            t = 3 * dy + dx
            cut = slice(dx * OC, (dx + 1) * OC)
            value = gm2[:, cut] * sd + gm_ref[dy, :, cut].astype(F32) * dsd + tap(k_ref, t) * cot_e
            out_ref[:, 16 * t : 16 * (t + 1)] = value.astype(BF16).reshape(NDP, 16, OC)


def sum_kernel(part_ref, target_ref, out_ref, new_ref):
    lengths = []
    for b in range(NDP):
        tile = part_ref[b, 144:152].astype(F32)
        lengths.append(tile[0:1] + tile[1:2] + tile[2:3])
    total = lengths[0]
    for b in range(1, NDP):
        total = total + lengths[b]
    old = target_ref[0]
    target = old + PL_DECAY * (total / NDP - old)
    new_ref[...] = jnp.broadcast_to(target, (8, OC))
    value = None
    for b in range(NDP):
        factor = 2.0 * PL_WEIGHT * (lengths[b] - target) / lengths[b]
        term = part_ref[b, 0:144].astype(F32) * factor
        value = term if value is None else value + term
    out_ref[...] = value.astype(BF16)


def last_kernel(z_ref, p0, p1, p2, p3, out_ref):
    z = z_ref[0]
    for k, p in enumerate((p0, p1, p2, p3)):
        at = pl.multiple_of(lax.rem(z + 4 - k, 4) * OC, OC)
        out_ref[:, pl.ds(at, OC)] = p[...].astype(F32)


def shape(dims, kind):
    return jax.ShapeDtypeStruct(dims, kind)


def call(kernel, outs, specs, mib, scratch=(), out_specs=None):
    return pl.pallas_call(
        kernel,
        out_shape=outs,
        in_specs=specs,
        out_specs=out_specs or jax.tree.map(lambda _: full(), outs),
        scratch_shapes=list(scratch),
        compiler_params=params(mib),
    )


def ring(x, axis, size):
    return [lax.ppermute(x, axis, [(i, (i + k) % size) for i in range(size)]) for k in range(1, size)]


def pinned(x):
    return pltpu.with_memory_space_constraint(x, pltpu.HBM)


def place(x, y, c):
    return ((x % 4) * 4 + y % 4) * 2 + c % 2


def permuted(value, to):
    return [
        lax.ppermute(
            value, "dp", [(place(x, y, c), place(*to(x, y, c, k))) for x in range(4) for y in range(4) for c in range(2)]
        )
        for k in range(1, 4)
    ]


def pack_kernel(z_ref, f_ref, d_hbm, k_ref, message_ref, mine_ref, d_ref, sems):
    lo = pl.multiple_of(z_ref[0] * OC, OC)
    copies = [
        pltpu.make_async_copy(f_ref, message_ref.at[pl.ds(0, 256)], sems.at[0]),
        pltpu.make_async_copy(k_ref.at[:, :, pl.ds(lo, OC)], mine_ref, sems.at[1]),
    ]
    marks = pltpu.make_async_copy(d_hbm, d_ref, sems.at[2])
    marks.start()
    for copy in copies:
        copy.start()
    marks.wait()
    rows = jnp.concatenate([d_ref[:, 0], d_ref[:, 1]], axis=1)
    high = rows.astype(BF16).astype(F32)
    middle = (rows - high).astype(BF16).astype(F32)
    low = (rows - high) - middle
    parts = jnp.concatenate([high, middle, low, jnp.zeros((7, 256), F32)], axis=0).astype(BF16)
    message_ref[256:272, :] = jnp.concatenate([parts, jnp.zeros((16, 256), BF16)], axis=1)
    for copy in copies:
        copy.wait()


def stack_kernel(step, p_ref, own, r1, r2, r3, *rest):
    out_ref = rest[-1]
    at = lax.rem(lax.div(p_ref[0], step), 4)
    for k, part in enumerate((own, r1, r2, r3)):
        out_ref[lax.rem(at + 4 - k, 4)] = part[...]


def stacked(place_of, step, own, parts, arrived):
    return call(
        functools.partial(stack_kernel, step),
        shape((4,) + own.shape, BF16),
        [full(SMEM)] + [full()] * 4 + [full(pl.ANY)] * len(arrived),
        8,
    )(place_of, own, *parts, *arrived)


def per_device(
    features, latent_bank, latent_ids, conv_kernel, style_one, bias_one, style_two, bias_two,
    rgb_weight, conv_bias, direction, length_target,
):
    zi = lax.axis_index("space")
    z = zi.reshape(1)
    di = lax.axis_index("dp").reshape(1)
    message, mine = call(
        pack_kernel,
        (shape((272, CH), BF16), shape((9, 16, OC), BF16)),
        [full(SMEM)] + [full(pltpu.HBM)] * 3,
        8,
        [VMEM((3, 2, COLS), F32), pltpu.SemaphoreType.DMA((3,))],
    )(
        z,
        pinned(features.reshape(256, CH)),
        pltpu.with_memory_space_constraint(direction.reshape(3, 2, COLS), pltpu.HBM),
        pltpu.with_memory_space_constraint(conv_kernel.reshape(9, 16, CH), pltpu.HBM),
    )
    others = ring(message, "space", 4)
    column = stacked(di, 2, mine, permuted(mine, lambda x, y, c, k: (x, y + k, c)), [])
    b1 = bias_one.reshape(1, CH)
    b2 = bias_two.reshape(1, CH)
    bias = conv_bias.reshape(1, CH)
    rgb = jnp.pad(rgb_weight.T, ((0, 5), (0, 0)))
    s, c, w1t, w2t = call(
        styles_kernel,
        (shape((1, CH), F32), shape((1, OC), F32), shape((CH, CH), F32), shape((OC, CH), F32)),
        [full(SMEM)] * 2 + [full(pltpu.HBM)] * 5,
        8,
        [
            VMEM((1, CH), F32),
            VMEM((CH, CH), F32),
            VMEM((CH, OC), F32),
            VMEM((1, CH), F32),
            VMEM((1, CH), F32),
            pltpu.SemaphoreType.DMA((5,)),
        ],
    )(z, latent_ids, pinned(latent_bank), pinned(style_one), pinned(b1), pinned(style_two), pinned(b2))
    image, turned, marks_all, marks_turned = call(
        image_kernel,
        (shape((NPOS, CH), BF16), shape((CH, NPOS), BF16), shape((16, NPOS), BF16), shape((NPOS, OC), BF16)),
        [full(SMEM)] + [full()] * 4,
        16,
    )(z, message, *others)
    plane = stacked(di, 8, column, permuted(column, lambda x, y, c, k: (x + k, y, c)), [s, marks_all])
    sibling = lax.ppermute(plane, "dp", [(i, i ^ 1) for i in range(NDP)])
    ga, half = call(
        ahead_kernel,
        (shape((NPOS, OC), BF16), shape((NDP // 2, 16, OC), F32)),
        [full(SMEM)] + [full()] * 4,
        8,
    )(z, marks_turned, c, rgb, plane)
    kernel, u, pre, gm, energy, rows = call(
        first_kernel,
        (
            shape((NDP, 9, 16, OC), BF16),
            shape((1, CH), F32),
            shape((NPOS, OC), F32),
            shape((3, CH, 3 * OC), BF16),
            shape((NDP, 16, OC), F32),
            shape((8, OC), F32),
        ),
        [full(SMEM)] * 2 + [full()] * 12,
        16,
    )(z, di, image, turned, marks_all, ga, half, plane, sibling, s, rgb, bias, w1t, w2t)
    parts, length = call(
        second_kernel,
        (pltpu.HBM((NDP, 152, OC), BF16), shape((8, OC), F32)),
        [full(SMEM)] + [full()] * 18,
        16,
        [VMEM((8, CH), F32)],
    )(
        z, u, *ring(u, "space", 4), image, turned, marks_turned, kernel, s, rgb, bias, w1t, w2t,
        pre, ga, gm, energy, rows,
    )
    received = lax.all_to_all(parts, "dp", 0, 0, tiled=True)
    shard, target = call(
        sum_kernel,
        (shape((144, OC), BF16), shape((8, OC), F32)),
        [full(), full(SMEM)],
        8,
    )(received, length_target)
    kernel_grad = call(
        last_kernel,
        shape((144, CH), F32),
        [full(SMEM)] + [full()] * 4,
        16,
    )(z, shard, *ring(shard, "space", 4))
    return (kernel_grad.reshape(3, 3, 16, CH), length[0, 0:1], target[0, 0:1])


def solution(mesh):
    in_specs = (
        P("dp", "space", None, None),
        P(),
        P("dp"),
        P(None, None, "dp", None),
        P(),
        P(),
        P(),
        P(),
        P(),
        P(),
        P("dp", None, "space", None),
        P(),
    )
    out_specs = (P(None, None, "dp", None), P("dp"), P())
    return jax.shard_map(per_device, mesh=mesh, in_specs=in_specs, out_specs=out_specs, check_vma=False)
```
